256 devices in a mesh: stream: 4 (over y), cross: 64 (over x, z, core).
Axes of the slice: x: 4, y: 4, z: 8, core: 2. Of those that a mesh axis runs over, the one named last changes fastest.
Arguments:
- old_state: bfloat16 [4096, 8, 320], P(('stream', 'cross')), may hold values from -6 to 6
- right_side: bfloat16 [4096, 8, 320], P(('stream', 'cross')), may hold values from -6 to 6
- block_inverse: bfloat16 [4096, 320, 320], P(('stream', 'cross')), may hold values from -0.3125 to 0.3125
- face_scale: float32 [4096, 6], P(('stream', 'cross')), may hold values from 0.25 to 1
- sweep_level: int32 [4096], P(('stream', 'cross')), may hold values from 0 to 3
- face_source: int32 [4096, 6], P(('stream', 'cross')), may hold values from 0 to 160, as said below
- send_list: int32 [4, 64, 2, 16], P('stream', 'cross'), may hold values from 0 to 96, as said below
- trace_map: bfloat16 [320, 480], replicated, may hold values from -0.3125 to 0.3125
- lift_map: bfloat16 [480, 320], replicated, may hold values from -0.25 to 0.25
Outputs:
- new_state: bfloat16 [4096, 8, 320], P(('stream', 'cross'))
The draws below stay inside these ranges and needn't reach their ends.
Inputs may be any that keep to these rules, and one draw needn't show every extreme that they name: `face_source`: indexes the rows of its own partition's table. `send_list`: 96 marks an empty slot; empty slots follow the live ones in each list; some list has all 16 slots live.
All inputs are finite; a program needn't handle non-finite values.
Results may differ from the reference program's by a relative error of at most 0.012.
Values may be sent and summed in bfloat16 or wider, within the bound.
No kernel may reach another device: no remote copies, remote signals or barrier semaphores. Data moves between devices by JAX's collectives and lax.ppermute only.
A program may use at most 64 MiB of HBM per device.

```python
import math
import jax
import jax.numpy as jnp

NP = 320
NT = 80
NF = 6
RHS = 8
LEVELS = 4
E_DEV = 16
CAP = 16
ELEMENTS = 4096
N_STREAM = 4
N_CROSS = 64


def draw_face_source(key, part):
    key_pick, key_local, key_along, key_cross = jax.random.split(key, 4)
    shape = (ELEMENTS, NF)
    picker = jax.random.randint(key_pick, shape, 0, 10)
    local_row = jax.random.randint(key_local, shape, 0, E_DEV * NF)
    along_row = jax.random.randint(key_along, shape, 0, E_DEV)
    cross_row = jax.random.randint(key_cross, shape, 0, 2 * CAP)
    face_ids = jnp.arange(NF)[None, :]
    zero_index = E_DEV * NF + 2 * E_DEV + 2 * CAP
    streamwise = jnp.where(face_ids == 0, E_DEV * NF + along_row, E_DEV * NF + E_DEV + along_row)
    remote = jnp.where(face_ids < 2, streamwise, E_DEV * NF + 2 * E_DEV + cross_row)
    limit = jnp.where(face_ids < 2, 7, 5)
    return jnp.where(picker < limit, remote, jnp.where(picker < 9, local_row, zero_index)).astype(jnp.int32)


def draw_send_list(key, part):
    key_count, key_full, key_value = jax.random.split(key, 3)
    counts = jax.random.randint(key_count, (N_STREAM, N_CROSS, 2), 1, CAP + 1)
    flat_ids = jnp.arange(N_STREAM * N_CROSS * 2).reshape(N_STREAM, N_CROSS, 2)
    full_one = jax.random.randint(key_full, (), 0, N_STREAM * N_CROSS * 2)
    counts = jnp.where(flat_ids == full_one, CAP, counts)
    values = jax.random.randint(key_value, (N_STREAM, N_CROSS, 2, CAP), 0, E_DEV * NF)
    slot_ids = jnp.arange(CAP)[None, None, None, :]
    return jnp.where(slot_ids < counts[:, :, :, None], values, E_DEV * NF).astype(jnp.int32)


def with_ends(array, rng, least, top_value):
    spot = [jax.random.randint(jax.random.fold_in(rng, axis), (), 0, length) for axis, length in enumerate(array.shape)]
    main_axis = array.shape.index(max(array.shape))
    neighbour = spot[:main_axis] + [(spot[main_axis] + 1) % array.shape[main_axis]] + spot[main_axis + 1:]
    return array.at[tuple(spot)].set(least).at[tuple(neighbour)].set(top_value)


def block_levels(stream_key, dims, cuts, low, top_value):
    def one(dim, blocks):
        steps = jax.random.uniform(jax.random.fold_in(jax.random.fold_in(stream_key, 6), dim), (blocks,), jnp.float32, low / len(cuts), top_value / len(cuts))
        return jnp.repeat(jnp.exp(steps), dims[dim] // blocks).reshape((-1,) + (1,) * (len(dims) - dim - 1))

    factor_of = one(*cuts[0])
    for cut in cuts[1:]:
        factor_of = factor_of * one(*cut)
    return factor_of


def bell_draw(stream_key, extent, width, most, shards=(), held_as=jnp.bfloat16):
    factor_of = block_levels(stream_key, extent, shards, -0.22, 0.18) if shards else 1.0
    entries = jax.random.normal(stream_key, extent, jnp.float32) * width * factor_of
    return jnp.minimum(jnp.maximum(entries, -most), most).astype(held_as)


def setup_inputs(seed: int = 0) -> dict:
    splits = jax.random.split(jax.random.key(seed), 10)
    old_state = bell_draw(splits[0], (ELEMENTS, RHS, NP), 1.0, 6.0, ((0, 256),))
    right_side = bell_draw(splits[1], (ELEMENTS, RHS, NP), 1.0, 6.0, ((0, 256),))
    block_inverse = bell_draw(splits[2], (ELEMENTS, NP, NP), NP ** -0.5, 0.3125, ((0, 256),))
    face_scale = jnp.clip(jnp.exp(math.log(1.0) - 1.3862944 * jax.random.uniform(splits[3], (ELEMENTS, NF), jnp.float32) ** block_levels(splits[3], (ELEMENTS, NF), ((0, 256),), -0.2, 0.2)), 0.25, 1.0)
    sweep_level = with_ends(jax.random.randint(splits[4], (ELEMENTS,), 0, LEVELS), jax.random.fold_in(splits[4], 1), 0, LEVELS - 1).astype(jnp.int32)
    face_source = draw_face_source(jax.random.fold_in(splits[9], 71), 0)
    send_list = draw_send_list(jax.random.fold_in(splits[9], 71), 0)
    trace_map = bell_draw(splits[7], (NP, NF * NT), NP ** -0.5, 0.3125)
    lift_map = bell_draw(splits[8], (NF * NT, NP), (NF * NT) ** -0.5, 0.25)
    return {"old_state": old_state, "right_side": right_side, "block_inverse": block_inverse, "face_scale": face_scale, "sweep_level": sweep_level, "face_source": face_source, "send_list": send_list, "trace_map": trace_map, "lift_map": lift_map}


def face_traces(blocks, trace_map, face_idx):
    elem_count, rhs_count, points = blocks.shape
    columns = trace_map[:, face_idx * NT:(face_idx + 1) * NT]
    product = jnp.dot(blocks.reshape(elem_count * rhs_count, points), columns, preferred_element_type=jnp.float32)
    return product.reshape(elem_count, rhs_count * NT).astype(jnp.bfloat16)


def element_traces(blocks, trace_map):
    elem_count, rhs_count, points = blocks.shape
    product = jnp.dot(blocks.reshape(elem_count * rhs_count, points), trace_map, preferred_element_type=jnp.float32)
    product = product.reshape(elem_count, rhs_count, NF, NT).transpose(0, 2, 1, 3)
    return product.reshape(elem_count * NF, rhs_count * NT).astype(jnp.bfloat16)


def update_blocks(right_rows, gathered, face_scale, lift_map, block_inverse):
    elem_count, rhs_count, points = right_rows.shape
    gathered = gathered.reshape(elem_count, NF, rhs_count, NT)
    scaled = (face_scale[:, :, None, None] * gathered.astype(jnp.float32)).astype(jnp.bfloat16)
    scaled = scaled.transpose(0, 2, 1, 3).reshape(elem_count * rhs_count, NF * NT)
    lifted = jnp.dot(scaled, lift_map, preferred_element_type=jnp.float32).reshape(elem_count, rhs_count, points)
    residual = (right_rows.astype(jnp.float32) - lifted).astype(jnp.bfloat16)
    updated = jnp.einsum("epq,erq->erp", block_inverse.astype(jnp.float32), residual.astype(jnp.float32))
    return updated.astype(jnp.bfloat16)


def pick_rows(source, indices):
    return source[indices]


def reference(old_state, right_side, block_inverse, face_scale, sweep_level, face_source, send_list, trace_map, lift_map):
    streams = N_STREAM
    parts = N_CROSS
    row_width = RHS * NT
    current = old_state.reshape(streams, parts * E_DEV, RHS, NP)
    right_all = right_side.reshape(streams, parts * E_DEV, RHS, NP)
    inverse_all = block_inverse.reshape(streams, parts * E_DEV, NP, NP)
    scale_all = face_scale.reshape(streams, parts * E_DEV, NF)
    level_all = sweep_level.reshape(streams, parts * E_DEV)
    source_all = face_source.reshape(streams, parts, E_DEV * NF)
    zero_rows = jnp.zeros((parts, E_DEV, row_width), jnp.bfloat16)
    zero_row = jnp.zeros((parts, 1, row_width), jnp.bfloat16)
    for section_idx in range(streams):
        if section_idx > 0:
            upstream = face_traces(current[section_idx - 1], trace_map, 1).reshape(parts, E_DEV, row_width)
        else:
            upstream = zero_rows
        if section_idx < streams - 1:
            downstream = face_traces(current[section_idx + 1], trace_map, 0).reshape(parts, E_DEV, row_width)
        else:
            downstream = zero_rows
        for level_idx in range(LEVELS):
            blocks = current[section_idx]
            own_traces = element_traces(blocks, trace_map).reshape(parts, E_DEV * NF, row_width)
            padded = jnp.concatenate([own_traces, zero_row], 1)
            outbound = jax.vmap(pick_rows)(padded, send_list[section_idx].reshape(parts, 2 * CAP))
            from_left = jnp.roll(outbound[:, CAP:], 1, axis=0)
            from_right = jnp.roll(outbound[:, :CAP], -1, axis=0)
            trace_table = jnp.concatenate([own_traces, upstream, downstream, from_left, from_right, zero_row], 1)
            gathered = jax.vmap(pick_rows)(trace_table, source_all[section_idx])
            updated = update_blocks(right_all[section_idx], gathered.reshape(parts * E_DEV * NF, row_width),
                                    scale_all[section_idx], lift_map, inverse_all[section_idx])
            chosen = level_all[section_idx] == level_idx
            current = current.at[section_idx].set(jnp.where(chosen[:, None, None], updated, blocks))
    return current.reshape(ELEMENTS, RHS, NP)
```

```python
import functools

import jax
import jax.numpy as jnp
from jax import lax
from jax.experimental import pallas as pl
from jax.experimental.pallas import tpu as pltpu
from jax.sharding import PartitionSpec as P

NT = 80
NF = 6
RHS = 8
LEVELS = 4
GROUPS = 10
BF = jnp.bfloat16
F32 = jnp.float32


def dot(a, b):
    return jnp.dot(a, b, preferred_element_type=F32)


def own_groups(maps, state):
    rows = dot(maps, state).astype(BF)
    return jnp.concatenate([rows[f * NT : (f + 1) * NT] for f in range(NF)], axis=1)


def own_column(row):
    item = (row * 43) >> 8
    return (row - item * NF) * 128 + item * RHS


def prepare(
    place, state, right, source, send, scale, level, trace_map, lift_map,
    pick, pick_out, scales, levels, state_t, right_t, trace_t, lift_t, own, to_core, to_chip,
):
    section, sections, odd = place[0], place[1], place[2]
    count = source.shape[0]
    width = count * RHS
    spread = (
        lax.broadcasted_iota(jnp.int32, (count, width), 1) // RHS
        == lax.broadcasted_iota(jnp.int32, (count, width), 0)
    )
    rhs = lax.broadcasted_iota(jnp.int32, (1, width), 1) % RHS

    def along(column):
        zero = jnp.zeros((count, width), column.dtype)
        return jnp.where(spread, jnp.broadcast_to(column, (count, width)), zero).sum(0, keepdims=True)

    levels[...] = jnp.broadcast_to(along(level[...]), levels.shape)
    left_group = jnp.where(odd == 1, 8, 9)
    right_group = jnp.where(odd == 1, 9, 8)
    upstream = jnp.where(section > 0, 6, -1000)
    downstream = jnp.where(section < sections - 1, 7, -1000)
    faces = source[...]
    weights = scale[...]
    for f in range(NF):
        row = along(faces[:, f : f + 1])
        column = own_column(row)
        for start, group in ((96, upstream), (112, downstream), (128, left_group), (144, right_group)):
            column = jnp.where(row >= start, group * 128 + (row - start) * RHS, column)
        column = jnp.where(row >= 160, -1000, column) + rhs
        at = lax.broadcasted_iota(jnp.int32, (GROUPS * 128, width), 0)
        pick[:, f * 128 : (f + 1) * 128] = jnp.where(at == column, 1.0, 0.0).astype(BF)
        scales[f * NT : (f + 1) * NT] = jnp.broadcast_to(along(weights[:, f : f + 1]), (NT, width))
    lists = dot(send[...].astype(F32).astype(BF), jnp.where(spread, 1.0, 0.0).astype(BF)).astype(jnp.int32)
    lower, higher = lists[0:1], lists[1:2]
    for k, row in enumerate((jnp.where(odd == 1, lower, higher), jnp.where(odd == 1, higher, lower))):
        column = jnp.where(row >= 96, -1000, own_column(row)) + rhs
        at = lax.broadcasted_iota(jnp.int32, (NF * 128, width), 0)
        pick_out[:, k * 128 : (k + 1) * 128] = jnp.where(at == column, 1.0, 0.0).astype(BF)
    state_t[...] = state[...].astype(F32).T.astype(BF)
    right_t[...] = right[...].astype(F32).T
    trace_t[...] = trace_map[...].astype(F32).T.astype(BF)
    lift_t[...] = lift_map[...].astype(F32).T.astype(BF)
    table = own_groups(trace_t[...], state_t[...])
    own[...] = table
    out = dot(table, pick_out[...]).astype(BF)
    to_core[...] = out[:, :128]
    to_chip[...] = out[:, 128:]


def visit(
    section, level_idx, last, place, state_t, own, up, down, from_core, from_chip,
    pick, pick_out, scales, levels, right_t, trace_t, lift_t, inverse, *outs,
):
    count, points = inverse.shape[0], inverse.shape[1]
    active = place[0] == section
    end = level_idx == LEVELS - 1
    new_state = outs[0]

    @pl.when(active)
    def _():
        table = jnp.concatenate(
            [own[...], up[...], down[...], from_core[...], from_chip[...]], axis=1
        )
        gathered = dot(table, pick[...])
        scaled = jnp.concatenate(
            [
                (scales[f * NT : (f + 1) * NT] * gathered[:, f * 128 : (f + 1) * 128]).astype(BF)
                for f in range(NF)
            ],
            axis=0,
        )
        residual = (right_t[...] - dot(lift_t[...], scaled)).astype(BF)
        item = lax.broadcasted_iota(jnp.int32, (1, residual.shape[1]), 1) // RHS
        item = jnp.where(levels[0:1] == level_idx, item, -1)
        state = state_t[...].astype(F32)
        for e in range(count):
            state = jnp.where(item == e, dot(inverse[e], residual), state)
        state = state.astype(BF)
        new_state[...] = state.astype(F32).T.astype(BF) if last else state
        if last:
            pass
        elif end:
            outs[1][...] = dot(trace_t[NT : 2 * NT], state).astype(BF)
        else:
            fresh = own_groups(trace_t[...], state)
            outs[1][...] = fresh
            out = dot(fresh, pick_out[...]).astype(BF)
            outs[2][...] = out[:, :128]
            outs[3][...] = out[:, 128:]

    @pl.when(jnp.logical_not(active))
    def _():
        new_state[...] = state_t[...].astype(F32).T.astype(BF) if last else state_t[...]
        if not last and not end:
            outs[1][...] = own[...]


VMEM = pl.BlockSpec(memory_space=pltpu.VMEM)
SMEM = pl.BlockSpec(memory_space=pltpu.SMEM)


def call(body, arrays, shapes, name):
    return pl.pallas_call(
        body,
        out_shape=[jax.ShapeDtypeStruct(s, d) for s, d in shapes],
        in_specs=[SMEM] + [VMEM] * (len(arrays) - 1),
        out_specs=[VMEM] * len(shapes),
        compiler_params=pltpu.CompilerParams(vmem_limit_bytes=24 * 2**20),
        name=name,
    )(*arrays)


def on_device(
    old_state, right_side, block_inverse, face_scale, sweep_level, face_source, send_list, trace_map, lift_map
):
    count, rhs, points = old_state.shape
    width = count * rhs
    traces = NF * NT
    sections, parts = lax.axis_size("stream"), lax.axis_size("cross")
    axes = ("stream", "cross")
    place = jnp.stack(
        [lax.axis_index("stream"), jnp.int32(sections), lax.axis_index("cross") % 2]
    ).astype(jnp.int32)

    def swap(array, stream_of, cross_of):
        pairs = [
            (s * parts + c, stream_of(s) * parts + cross_of(s, c)) for s in range(sections) for c in range(parts)
        ]
        return lax.ppermute(array, axes, pairs)

    def core(c):
        return c ^ 1

    def chip(c):
        return (c + 1) % parts if c % 2 else (c - 1) % parts

    def exchange(to_core, to_chip, section=None):
        def within(move):
            return lambda s, c: move(c) if section is None or s == section else c

        far = swap(to_chip, lambda s: s, within(chip))
        near = swap(to_core, lambda s: s, within(core))
        return near, far

    group = ((NT, width), BF)
    prepared = call(
        prepare,
        (place, old_state.reshape(width, points), right_side.reshape(width, points), face_source,
         send_list.reshape(2, count), face_scale, sweep_level.reshape(count, 1), trace_map, lift_map),
        [((GROUPS * 128, NF * 128), BF), ((NF * 128, 256), BF), ((traces, width), F32), ((8, width), jnp.int32),
         ((points, width), BF), ((points, width), F32), ((traces, points), BF), ((points, traces), BF),
         ((NT, NF * 128), BF), group, group],
        "prepare",
    )
    pick, pick_out, scales, levels, state, right_t, trace_t, lift_t, own, to_core, to_chip = prepared
    first_core, first_chip = exchange(to_core, to_chip)
    down = swap(own[:, :128], lambda s: (s - 1) % sections, lambda s, c: c)
    up = down
    for section in range(sections):
        from_core, from_chip = first_core, first_chip
        for level_idx in range(LEVELS):
            end = level_idx == LEVELS - 1
            last = end and section == sections - 1
            shapes = [((width, points) if last else (points, width), BF)]
            if end and not last:
                shapes.append(group)
            elif not end:
                shapes += [((NT, NF * 128), BF), group, group]
            outs = call(
                functools.partial(visit, section, level_idx, last),
                (place, state, own, up, down, from_core, from_chip,
                 pick, pick_out, scales, levels, right_t, trace_t, lift_t, block_inverse),
                shapes,
                "visit",
            )
            state = outs[0]
            if not end:
                own = outs[1]
                from_core, from_chip = exchange(outs[2], outs[3], section)
            elif not last:
                pair = {section: section + 1, section + 1: section}
                up = swap(outs[1], lambda s: pair.get(s, s), lambda s, c: c)
    return state.reshape(count, rhs, points)


def solution(mesh):
    return jax.shard_map(
        on_device,
        mesh=mesh,
        in_specs=(
            P(("stream", "cross"), None, None),
            P(("stream", "cross"), None, None),
            P(("stream", "cross"), None, None),
            P(("stream", "cross"), None),
            P(("stream", "cross")),
            P(("stream", "cross"), None),
            P("stream", "cross", None, None),
            P(),
            P(),
        ),
        out_specs=P(("stream", "cross"), None, None),
        check_vma=False,
    )
```

```python
import functools

import jax
import jax.numpy as jnp
from jax import lax
from jax.experimental import pallas as pl
from jax.experimental.pallas import tpu as pltpu
from jax.sharding import PartitionSpec as P

NT = 80
NF = 6
RHS = 8
LEVELS = 4
CAP = 16
OWN = 96
ZERO = 160
LISTS = 6
LEVEL_ROW = 8
PLACE_ROW = 9
BF = jnp.bfloat16
F32 = jnp.float32


def dot(a, b):
    return jnp.dot(a, b, preferred_element_type=F32)


def rounded(a):
    return a.astype(BF).astype(F32)


def block(index):
    return pl.ds(pl.multiple_of(index * RHS, RHS), RHS)


def store_own(own, state, traces):
    count = state.shape[0] // RHS
    own[OWN * RHS :] = jnp.zeros((RHS, NT), F32)
    for f in range(NF):
        rows = rounded(dot(state, traces[f]))
        for e in range(count):
            at = (e * NF + f) * RHS
            own[at : at + RHS] = rows[e * RHS : (e + 1) * RHS]


def store_sent(own, meta, *messages):
    for k, message in enumerate(messages):
        for q in range(0, CAP, 2):
            pair = [own[block(meta[LISTS + k, q + j]), :] for j in range(2)]
            message[q * RHS : (q + 2) * RHS] = jnp.concatenate(pair, axis=0).astype(BF)


def prepare(
    place, old_state, trace_map, source, scale, send, level,
    meta, weights, state, traces, own, to_core, to_chip, face0,
):
    count = level.shape[1]
    at = place[...]
    section, sections, odd = at[0, 0], at[0, 1], at[0, 2]
    row = source[...]
    first, second = (row >= 128) & (row < 144), (row >= 144) & (row < 160)
    moved = jnp.where(first, row + CAP, jnp.where(second, row - CAP, row))
    row = jnp.where(odd == 1, row, moved)
    row = jnp.where((section == 0) & (row >= 96) & (row < 112), ZERO, row)
    row = jnp.where((section == sections - 1) & (row >= 112) & (row < 128), ZERO, row)
    lists = send[...]
    lower, higher = lists[0:1], lists[1:2]
    meta[...] = jnp.zeros(meta.shape, jnp.int32)
    meta[0:NF, 0:count] = row
    meta[LISTS : LISTS + 1, 0:CAP] = jnp.where(odd == 1, lower, higher)
    meta[LISTS + 1 : LISTS + 2, 0:CAP] = jnp.where(odd == 1, higher, lower)
    meta[LEVEL_ROW : LEVEL_ROW + 1, 0:count] = level[...]
    meta[PLACE_ROW : PLACE_ROW + 1] = jnp.full((1, meta.shape[1]), section, jnp.int32)
    weights[0:NF, 0:count] = scale[...]
    current = old_state[...]
    state[...] = current.astype(F32)
    for f in range(NF):
        traces[f] = trace_map[:, f * NT : (f + 1) * NT]
    store_own(own, current, traces)
    store_sent(own, meta[...], to_core, to_chip)
    face0[...] = dot(current, traces[0]).astype(BF)


def turn(inverse, lift_t, inverse_t, lift):
    for e in range(inverse.shape[0]):
        inverse_t[e] = inverse[e].T
    lift[...] = lift_t[...].T


def visit(
    section, level_idx, last, meta_ref, weights_ref, state, own, up, down, from_core, from_chip,
    right, traces, lift, inverse_t, *rest,
):
    *outs, table, scaled, fresh = rest
    count = inverse_t.shape[0]
    end = level_idx == LEVELS - 1
    meta = meta_ref[...]
    active = meta[PLACE_ROW, 0] == section

    @pl.when(active)
    def _():
        weights = weights_ref[...]
        table[0 : OWN * RHS] = own[0 : OWN * RHS]
        for k, part in enumerate((up, down, from_core, from_chip)):
            start = (OWN + k * CAP) * RHS
            table[start : start + CAP * RHS] = part[...].astype(F32)
        table[ZERO * RHS :] = jnp.zeros((RHS, NT), F32)
        for f in range(NF):
            for e in range(count):
                scaled[f, e * RHS : (e + 1) * RHS] = weights[f, e] * table[block(meta[f, e]), :]
        lifted = dot(scaled[0].astype(BF), lift[0:NT])
        for f in range(1, NF):
            lifted = lifted + dot(scaled[f].astype(BF), lift[f * NT : (f + 1) * NT])
        residual = rounded(right[...].astype(F32) - lifted)
        for e in range(count):
            rows = slice(e * RHS, (e + 1) * RHS)
            update = rounded(dot(residual[rows].astype(BF), inverse_t[e]))
            fresh[rows] = jnp.where(meta[LEVEL_ROW, e] == level_idx, update, state[rows])
        current = fresh[...].astype(BF)
        outs[0][...] = current if last else fresh[...]
        if last:
            pass
        elif end:
            outs[1][...] = dot(current, traces[1]).astype(BF)
        else:
            store_own(outs[1], current, traces)
            store_sent(outs[1], meta, outs[2], outs[3])

    @pl.when(jnp.logical_not(active))
    def _():
        outs[0][...] = state[...].astype(BF) if last else state[...]
        if not last and not end:
            outs[1][...] = own[...]


VMEM = pl.BlockSpec(memory_space=pltpu.VMEM)


def call(body, arrays, shapes, name, scratch=()):
    return pl.pallas_call(
        body,
        out_shape=[jax.ShapeDtypeStruct(s, d) for s, d in shapes],
        in_specs=[VMEM] * len(arrays),
        out_specs=[VMEM] * len(shapes),
        scratch_shapes=[pltpu.VMEM(s, d) for s, d in scratch],
        compiler_params=pltpu.CompilerParams(vmem_limit_bytes=24 * 2**20),
        name=name,
    )(*arrays)


def on_device(
    old_state, right_side, block_inverse, face_scale, sweep_level, face_source, send_list, trace_map, lift_map
):
    count, rhs, points = old_state.shape
    rows = count * rhs
    sections, parts = lax.axis_size("stream"), lax.axis_size("cross")
    axes = ("stream", "cross")
    place = jnp.stack(
        [lax.axis_index("stream"), jnp.int32(sections), lax.axis_index("cross") % 2]
    ).astype(jnp.int32).reshape(1, 3)

    def core(c):
        return c ^ 1

    def chip(c):
        return (c + 1) % parts if c % 2 else (c - 1) % parts

    def move(array, target):
        pairs = []
        for s in range(sections):
            for c in range(parts):
                to_s, to_c = target(s, c)
                pairs.append((s * parts + c, to_s * parts + to_c))
        return lax.ppermute(array, axes, pairs)

    def between(array, pair_of):
        def target(s, c):
            other = pair_of(s)
            return (other, c) if 0 <= other < sections and other != s else (s, core(c))

        return move(array, target)

    def exchange(to_core, to_chip, section=None):
        far = move(to_chip, lambda s, c: (s, chip(c) if section in (None, s) else core(c)))
        near = move(to_core, lambda s, c: (s, core(c)))
        return near, far

    message = ((CAP * rhs, NT), BF)
    held = ((rows, points), F32)
    table = (((OWN + 1) * rhs, NT), F32)
    meta, weights, state, traces, own, to_core, to_chip, face0 = call(
        prepare,
        (place, old_state.reshape(rows, points), trace_map, face_source.T, face_scale.T,
         send_list.reshape(2, CAP), sweep_level.reshape(1, count)),
        [((16, 128), jnp.int32), ((8, 128), F32), held, ((NF, points, NT), BF), table, message, message, message],
        "prepare",
    )
    first_core, first_chip = exchange(to_core, to_chip)
    inverse_t, lift = call(
        turn,
        (block_inverse, lift_map.T),
        [(block_inverse.shape, BF), (lift_map.shape, BF)],
        "turn",
    )
    right = right_side.reshape(rows, points)
    even_down = between(face0, lambda s: s ^ 1)
    odd_down = between(face0, lambda s: s + 1 if s % 2 else s - 1)
    up = face0
    for section in range(sections):
        from_core, from_chip = first_core, first_chip
        down = odd_down if section % 2 else even_down
        for level_idx in range(LEVELS):
            end = level_idx == LEVELS - 1
            last = end and section == sections - 1
            shapes = [((rows, points), BF) if last else held]
            if end and not last:
                shapes.append(message)
            elif not end:
                shapes += [table, message, message]
            outs = call(
                functools.partial(visit, section, level_idx, last),
                (meta, weights, state, own, up, down, from_core, from_chip, right, traces, lift, inverse_t),
                shapes,
                "visit",
                scratch=[(((ZERO + 1) * rhs, NT), F32), ((NF, rows, NT), F32), held],
            )
            state = outs[0]
            if not end:
                own = outs[1]
                from_core, from_chip = exchange(outs[2], outs[3], section)
            elif not last:
                pair = {section: section + 1, section + 1: section}
                up = between(outs[1], lambda s: pair.get(s, s))
    return state.reshape(count, rhs, points)


def solution(mesh):
    return jax.shard_map(
        on_device,
        mesh=mesh,
        in_specs=(
            P(("stream", "cross"), None, None),
            P(("stream", "cross"), None, None),
            P(("stream", "cross"), None, None),
            P(("stream", "cross"), None),
            P(("stream", "cross")),
            P(("stream", "cross"), None),
            P("stream", "cross", None, None),
            P(),
            P(),
        ),
        out_specs=P(("stream", "cross"), None, None),
        check_vma=False,
    )
```

```python
import functools

import jax
import jax.numpy as jnp
from jax import lax
from jax.experimental import pallas as pl
from jax.experimental.pallas import tpu as pltpu
from jax.sharding import PartitionSpec as P

NT = 80
NF = 6
RHS = 8
LEVELS = 4
CAP = 16
OWN = 96
ZERO = 160
LISTS = 6
LEVEL_ROW = 8
PLACE_ROW = 9
GHOST_ROWS = 10
FACE1_AT = 384
BF = jnp.bfloat16
F32 = jnp.float32


def dot(a, b):
    return jnp.dot(a, b, preferred_element_type=F32)


def rounded(a):
    return a.astype(BF).astype(F32)


def block(index):
    return pl.ds(pl.multiple_of(index * RHS, RHS), RHS)


def store_own(own, state, traces):
    count = state.shape[0] // RHS
    own[OWN * RHS :] = jnp.zeros((RHS, NT), F32)
    for f in range(NF):
        rows = rounded(dot(state, traces[f]))
        for e in range(count):
            at = (e * NF + f) * RHS
            own[at : at + RHS] = rows[e * RHS : (e + 1) * RHS]


def store_sent(own, meta, *messages):
    for k, message in enumerate(messages):
        for q in range(0, CAP, 2):
            pair = [own[block(meta[LISTS + k, q + j]), :] for j in range(2)]
            message[q * RHS : (q + 2) * RHS] = jnp.concatenate(pair, axis=0).astype(BF)


def prepare(
    place, old_state, trace_map, source, scale, send, level,
    meta, weights, state, traces, own, to_core, to_chip, face0,
):
    count = level.shape[1]
    at = place[...]
    section, sections, odd = at[0, 0], at[0, 1], at[0, 2]
    row = source[...]
    first, second = (row >= 128) & (row < 144), (row >= 144) & (row < 160)
    moved = jnp.where(first, row + CAP, jnp.where(second, row - CAP, row))
    row = jnp.where(odd == 1, row, moved)
    row = jnp.where((section == 0) & (row >= 96) & (row < 112), ZERO, row)
    row = jnp.where((section == sections - 1) & (row >= 112) & (row < 128), ZERO, row)
    lists = send[...]
    lower, higher = lists[0:1], lists[1:2]
    meta[...] = jnp.zeros(meta.shape, jnp.int32)
    meta[0:NF, 0:count] = row
    meta[GHOST_ROWS : GHOST_ROWS + NF, 0:count] = jnp.where(row < 128, ZERO, row)
    meta[LISTS : LISTS + 1, 0:CAP] = jnp.where(odd == 1, lower, higher)
    meta[LISTS + 1 : LISTS + 2, 0:CAP] = jnp.where(odd == 1, higher, lower)
    meta[LEVEL_ROW : LEVEL_ROW + 1, 0:count] = level[...]
    meta[PLACE_ROW : PLACE_ROW + 1] = jnp.full((1, meta.shape[1]), section, jnp.int32)
    weights[0:NF, 0:count] = scale[...]
    current = old_state[...]
    state[...] = current.astype(F32)
    for f in range(NF):
        traces[f] = trace_map[:, f * NT : (f + 1) * NT]
    store_own(own, current, traces)
    store_sent(own, meta[...], to_core, to_chip)
    face0[...] = dot(current, traces[0]).astype(BF)


def turn(inverse, lift_t, traces, inverse_t, lift, lead):
    face1 = traces[1].T
    for e in range(inverse.shape[0]):
        inverse_t[e] = inverse[e].T
        lead[e * NT : (e + 1) * NT, 0 : inverse.shape[2]] = dot(face1, inverse[e]).astype(BF)
    lift[...] = lift_t[...].T


def fill(table, start, parts):
    for k, part in enumerate(parts):
        at = (start + k * CAP) * RHS
        table[at : at + CAP * RHS] = part[...].astype(F32)


def lifted(scaled, table, lift, meta, weights, count, first=0):
    table[ZERO * RHS :] = jnp.zeros((RHS, NT), F32)
    for f in range(NF):
        for e in range(count):
            scaled[f, e * RHS : (e + 1) * RHS] = weights[f, e] * table[block(meta[first + f, e]), :]
    total = dot(scaled[0].astype(BF), lift[0:NT])
    for f in range(1, NF):
        total = total + dot(scaled[f].astype(BF), lift[f * NT : (f + 1) * NT])
    return total


def visit(
    section, level_idx, meta_ref, weights_ref, state, own, up, down, from_core, from_chip,
    right, traces, lift, inverse_t, *rest,
):
    final = section is None
    gather_all = not final and level_idx == LEVELS - 2
    *outs, table, scaled, fresh = rest
    count = inverse_t.shape[0]
    points = lift.shape[1]
    meta = meta_ref[...]

    def step():
        fill(table, OWN, (up,))
        table[0 : OWN * RHS] = own[0 : OWN * RHS]
        fill(table, OWN + CAP, (down, from_core, from_chip))
        residual = rounded(
            right[...].astype(F32) - lifted(scaled, table, lift, meta, weights_ref[...], count)
        )
        for e in range(count):
            rows = slice(e * RHS, (e + 1) * RHS)
            update = rounded(dot(residual[rows].astype(BF), inverse_t[e]))
            fresh[rows] = jnp.where(meta[LEVEL_ROW, e] == level_idx, update, state[rows])
        current = fresh[...].astype(BF)
        if final:
            outs[0][...] = current
        else:
            outs[0][...] = fresh[...]
            store_own(outs[1], current, traces)
            store_sent(outs[1], meta, outs[2], outs[3])

    if final:
        step()
        return
    active = meta[PLACE_ROW, 0] == section
    pl.when(active)(step)

    @pl.when(jnp.logical_not(active))
    def _():
        outs[0][...] = state[...]
        outs[1][...] = own[...]
        if gather_all:
            store_sent(own, meta, outs[2], outs[3])


def upstream(
    section, meta_ref, up, carried, from_core, from_chip, there_ref, weights_ref, lead, lift, out, table, scaled
):
    active = meta_ref[...][PLACE_ROW, 0] == section
    points = lift.shape[1]
    count = lead.shape[0] // NT

    @pl.when(active)
    def _():
        there = there_ref[...]
        fill(table, 128, (from_core, from_chip))
        part = carried[:, 0:points].astype(F32) - lifted(
            scaled, table, lift, there, weights_ref[...], count, GHOST_ROWS
        )
        part = rounded(part)
        before = carried[:, FACE1_AT : FACE1_AT + NT].astype(F32)
        for e in range(count):
            rows = slice(e * RHS, (e + 1) * RHS)
            update = lax.dot_general(
                part[rows].astype(BF),
                lead[e * NT : (e + 1) * NT, 0:points],
                (((1,), (1,)), ((), ())),
                preferred_element_type=F32,
            )
            table[rows] = jnp.where(there[LEVEL_ROW, e] == LEVELS - 1, rounded(update), before[rows])
        out[...] = table[0 : count * RHS].astype(BF)

    @pl.when(jnp.logical_not(active))
    def _():
        out[...] = up[...]


def carry(section, meta_ref, weights_ref, own, up, down, right, lift, out, table, scaled):
    count = right.shape[0] // RHS
    points = right.shape[1]
    meta = meta_ref[...]

    @pl.when(meta[PLACE_ROW, 0] == section)
    def _():
        table[0 : OWN * RHS] = own[0 : OWN * RHS]
        fill(table, OWN, (up, down))
        table[128 * RHS : ZERO * RHS] = jnp.zeros(((ZERO - 128) * RHS, NT), F32)
        part = right[...].astype(F32) - lifted(scaled, table, lift, meta, weights_ref[...], count)
        out[:, 0:points] = part.astype(BF)
        face1 = [own[(e * NF + 1) * RHS : (e * NF + 2) * RHS] for e in range(count)]
        out[:, FACE1_AT : FACE1_AT + NT] = jnp.concatenate(face1, axis=0).astype(BF)


VMEM = pl.BlockSpec(memory_space=pltpu.VMEM)


def call(body, arrays, shapes, name, scratch=()):
    return pl.pallas_call(
        body,
        out_shape=[jax.ShapeDtypeStruct(s, d) for s, d in shapes],
        in_specs=[VMEM] * len(arrays),
        out_specs=[VMEM] * len(shapes),
        scratch_shapes=[pltpu.VMEM(s, d) for s, d in scratch],
        compiler_params=pltpu.CompilerParams(vmem_limit_bytes=24 * 2**20),
        name=name,
    )(*arrays)


def on_device(
    old_state, right_side, block_inverse, face_scale, sweep_level, face_source, send_list, trace_map, lift_map
):
    count, rhs, points = old_state.shape
    rows = count * rhs
    sections, parts = lax.axis_size("stream"), lax.axis_size("cross")
    axes = ("stream", "cross")
    place = jnp.stack(
        [lax.axis_index("stream"), jnp.int32(sections), lax.axis_index("cross") % 2]
    ).astype(jnp.int32).reshape(1, 3)

    def core(c):
        return c ^ 1

    def chip(c):
        return (c + 1) % parts if c % 2 else (c - 1) % parts

    def move(array, target):
        pairs = []
        for s in range(sections):
            for c in range(parts):
                to_s, to_c = target(s, c)
                pairs.append((s * parts + c, to_s * parts + to_c))
        return lax.ppermute(array, axes, pairs)

    def between(array, pair_of, across=lambda c: c):
        def target(s, c):
            other = pair_of(s)
            return (other, across(c)) if 0 <= other < sections and other != s else (s, core(c))

        return move(array, target)

    def exchange(to_core, to_chip, section=None):
        far = move(to_chip, lambda s, c: (s, chip(c) if section in (None, s) else core(c)))
        near = move(to_core, lambda s, c: (s, core(c)))
        return near, far

    message = ((CAP * rhs, NT), BF)
    held = ((rows, points), F32)
    table = (((OWN + 1) * rhs, NT), F32)
    meta, weights, state, traces, own, to_core, to_chip, face0 = call(
        prepare,
        (place, old_state.reshape(rows, points), trace_map, face_source.T, face_scale.T,
         send_list.reshape(2, CAP), sweep_level.reshape(1, count)),
        [((16, 128), jnp.int32), ((8, 128), F32), held, ((NF, points, NT), BF), table, message, message, message],
        "prepare",
    )
    first_core, first_chip = exchange(to_core, to_chip)
    inverse_t, lift, lead = call(
        turn,
        (block_inverse, lift_map.T, traces),
        [(block_inverse.shape, BF), (lift_map.shape, BF), ((count * NT, -(-points // 128) * 128), BF)],
        "turn",
    )
    right = right_side.reshape(rows, points)
    even_down = between(face0, lambda s: s ^ 1)
    odd_down = between(face0, lambda s: s + 1 if s % 2 else s - 1)
    down = jnp.where(lax.axis_index("stream") % 2 == 1, odd_down, even_down)

    def onward(array):
        return move(array, lambda s, c: ((s + 1) % sections, c))

    up = face0
    whole = ((ZERO + 1) * rhs, NT), F32
    picked = (NF, rows, NT), F32
    for section in range(sections):
        from_core, from_chip = first_core, first_chip
        for level_idx in range(LEVELS - 1):
            shapes = [held, table, message, message]
            if section > 0 and level_idx == 0:
                (up,) = call(
                    functools.partial(upstream, section),
                    (meta, up, carried, up_core, up_chip, up_meta, up_weights, up_lead, lift),
                    [message],
                    "upstream",
                    scratch=[whole, picked],
                )
            arrays = (meta, weights, state, own, up, down, from_core, from_chip, right, traces, lift, inverse_t)
            outs = call(
                functools.partial(visit, section, level_idx), arrays, shapes, "visit", scratch=[whole, picked, held]
            )
            state, own = outs[0], outs[1]
            if level_idx < LEVELS - 2:
                if section == 0 and level_idx == 0:
                    lead, sent_meta, sent_weights, _ = lax.optimization_barrier((lead, meta, weights, own))
                    up_lead, up_meta, up_weights = onward(lead), onward(sent_meta), onward(sent_weights)
                from_core, from_chip = exchange(outs[2], outs[3], section)
                if section == 0 and level_idx == 0:
                    from_chip, up_meta, up_weights = lax.optimization_barrier((from_chip, up_meta, up_weights))
        if section < sections - 1:
            pair = {section: section + 1, section + 1: section}
            up_chip = between(outs[3], lambda s: pair.get(s, s), chip)
            up_core = between(outs[2], lambda s: pair.get(s, s), core)
            (part,) = call(
                functools.partial(carry, section),
                (meta, weights, own, up, down, right, lift),
                [((rows, 512), BF)],
                "carry",
                scratch=[whole, picked],
            )
            carried = between(part, lambda s: pair.get(s, s))
    from_core, from_chip = exchange(outs[2], outs[3])
    (state,) = call(
        functools.partial(visit, None, LEVELS - 1),
        (meta, weights, state, own, up, down, from_core, from_chip, right, traces, lift, inverse_t),
        [((rows, points), BF)],
        "visit",
        scratch=[whole, picked, held],
    )
    return state.reshape(count, rhs, points)


def solution(mesh):
    return jax.shard_map(
        on_device,
        mesh=mesh,
        in_specs=(
            P(("stream", "cross"), None, None),
            P(("stream", "cross"), None, None),
            P(("stream", "cross"), None, None),
            P(("stream", "cross"), None),
            P(("stream", "cross")),
            P(("stream", "cross"), None),
            P("stream", "cross", None, None),
            P(),
            P(),
        ),
        out_specs=P(("stream", "cross"), None, None),
        check_vma=False,
    )
```

```python
import functools

import jax
import jax.numpy as jnp
from jax import lax
from jax.experimental import pallas as pl
from jax.experimental.pallas import tpu as pltpu
from jax.sharding import PartitionSpec as P

NT = 80
NF = 6
RHS = 8
LEVELS = 4
CAP = 16
OWN = 96
ZERO = 160
LISTS = 6
LEVEL_ROW = 8
PLACE_ROW = 9
GHOST_ROWS = 10
FACE1_AT = 384
BF = jnp.bfloat16
F32 = jnp.float32


def dot(a, b):
    return jnp.dot(a, b, preferred_element_type=F32)


def rounded(a):
    return a.astype(BF).astype(F32)


def block(index):
    return pl.ds(pl.multiple_of(index * RHS, RHS), RHS)


def store_own(own, state, traces):
    count = state.shape[0] // RHS
    own[OWN * RHS :] = jnp.zeros((RHS, NT), F32)
    for f in range(NF):
        rows = rounded(dot(state, traces[f]))
        for e in range(count):
            at = (e * NF + f) * RHS
            own[at : at + RHS] = rows[e * RHS : (e + 1) * RHS]


def store_sent(own, meta, *messages):
    for k, message in enumerate(messages):
        for q in range(0, CAP, 2):
            pair = [own[block(meta[LISTS + k, q + j]), :] for j in range(2)]
            message[q * RHS : (q + 2) * RHS] = jnp.concatenate(pair, axis=0).astype(BF)


def prepare(
    place, old_state, trace_map, source, scale, send, level,
    meta, weights, state, traces, own, to_core, to_chip, face0,
):
    count = level.shape[1]
    at = place[...]
    section, sections, odd = at[0, 0], at[0, 1], at[0, 2]
    row = source[...]
    first, second = (row >= 128) & (row < 144), (row >= 144) & (row < 160)
    moved = jnp.where(first, row + CAP, jnp.where(second, row - CAP, row))
    row = jnp.where(odd == 1, row, moved)
    row = jnp.where((section == 0) & (row >= 96) & (row < 112), ZERO, row)
    row = jnp.where((section == sections - 1) & (row >= 112) & (row < 128), ZERO, row)
    lists = send[...]
    lower, higher = lists[0:1], lists[1:2]
    meta[...] = jnp.zeros(meta.shape, jnp.int32)
    meta[0:NF, 0:count] = row
    meta[GHOST_ROWS : GHOST_ROWS + NF, 0:count] = jnp.where(row < 128, ZERO, row)
    meta[LISTS : LISTS + 1, 0:CAP] = jnp.where(odd == 1, lower, higher)
    meta[LISTS + 1 : LISTS + 2, 0:CAP] = jnp.where(odd == 1, higher, lower)
    meta[LEVEL_ROW : LEVEL_ROW + 1, 0:count] = level[...]
    meta[PLACE_ROW : PLACE_ROW + 1] = jnp.full((1, meta.shape[1]), section, jnp.int32)
    weights[0:NF, 0:count] = scale[...]
    current = old_state[...]
    state[...] = current.astype(F32)
    for f in range(NF):
        traces[f] = trace_map[:, f * NT : (f + 1) * NT]
    store_own(own, current, traces)
    store_sent(own, meta[...], to_core, to_chip)
    face0[...] = dot(current, traces[0]).astype(BF)


def turn(inverse, lift_t, traces, inverse_t, lift, lead):
    face1 = traces[1].T
    for e in range(inverse.shape[0]):
        inverse_t[e] = inverse[e].T
        lead[e * NT : (e + 1) * NT, 0 : inverse.shape[2]] = dot(face1, inverse[e]).astype(BF)
    lift[...] = lift_t[...].T


def fill(table, start, parts):
    for k, part in enumerate(parts):
        at = (start + k * CAP) * RHS
        table[at : at + CAP * RHS] = part[...].astype(F32)


def lifted(scaled, table, lift, meta, weights, count, first=0):
    table[ZERO * RHS :] = jnp.zeros((RHS, NT), F32)
    for f in range(NF):
        for e in range(count):
            scaled[f, e * RHS : (e + 1) * RHS] = weights[f, e] * table[block(meta[first + f, e]), :]
    total = dot(scaled[0].astype(BF), lift[0:NT])
    for f in range(1, NF):
        total = total + dot(scaled[f].astype(BF), lift[f * NT : (f + 1) * NT])
    return total


def visit(
    section, level_idx, from_chip, from_core, meta_ref, weights_ref, state, own, up, down,
    right, traces, lift, inverse_t, *rest,
):
    final = section is None
    gather_all = not final and level_idx == LEVELS - 2
    *outs, table, scaled, fresh = rest
    count = inverse_t.shape[0]
    points = lift.shape[1]
    meta = meta_ref[...]

    def step():
        fill(table, OWN, (up,))
        table[0 : OWN * RHS] = own[0 : OWN * RHS]
        fill(table, OWN + CAP, (down, from_core, from_chip))
        residual = rounded(
            right[...].astype(F32) - lifted(scaled, table, lift, meta, weights_ref[...], count)
        )
        for e in range(count):
            rows = slice(e * RHS, (e + 1) * RHS)
            update = rounded(dot(residual[rows].astype(BF), inverse_t[e]))
            fresh[rows] = jnp.where(meta[LEVEL_ROW, e] == level_idx, update, state[rows])
        current = fresh[...].astype(BF)
        if final:
            outs[0][...] = current
        else:
            outs[0][...] = fresh[...]
            store_own(outs[1], current, traces)
            store_sent(outs[1], meta, outs[2], outs[3])

    if final:
        step()
        return
    active = meta[PLACE_ROW, 0] == section
    pl.when(active)(step)

    @pl.when(jnp.logical_not(active))
    def _():
        outs[0][...] = state[...]
        outs[1][...] = own[...]
        if gather_all:
            store_sent(own, meta, outs[2], outs[3])


def upstream(
    section, from_chip, carried, from_core, meta_ref, up, there_ref, weights_ref, lead, lift, out, table, scaled
):
    active = meta_ref[...][PLACE_ROW, 0] == section
    points = lift.shape[1]
    count = lead.shape[0] // NT

    @pl.when(active)
    def _():
        there = there_ref[...]
        fill(table, 128, (from_core, from_chip))
        part = carried[:, 0:points].astype(F32) - lifted(
            scaled, table, lift, there, weights_ref[...], count, GHOST_ROWS
        )
        part = rounded(part)
        before = carried[:, FACE1_AT : FACE1_AT + NT].astype(F32)
        for e in range(count):
            rows = slice(e * RHS, (e + 1) * RHS)
            update = lax.dot_general(
                part[rows].astype(BF),
                lead[e * NT : (e + 1) * NT, 0:points],
                (((1,), (1,)), ((), ())),
                preferred_element_type=F32,
            )
            table[rows] = jnp.where(there[LEVEL_ROW, e] == LEVELS - 1, rounded(update), before[rows])
        out[...] = table[0 : count * RHS].astype(BF)

    @pl.when(jnp.logical_not(active))
    def _():
        out[...] = up[...]


def carry(section, meta_ref, weights_ref, own, up, down, right, lift, out, table, scaled):
    count = right.shape[0] // RHS
    points = right.shape[1]
    meta = meta_ref[...]

    @pl.when(meta[PLACE_ROW, 0] == section)
    def _():
        table[0 : OWN * RHS] = own[0 : OWN * RHS]
        fill(table, OWN, (up, down))
        table[128 * RHS : ZERO * RHS] = jnp.zeros(((ZERO - 128) * RHS, NT), F32)
        part = right[...].astype(F32) - lifted(scaled, table, lift, meta, weights_ref[...], count)
        out[:, 0:points] = part.astype(BF)
        face1 = [own[(e * NF + 1) * RHS : (e * NF + 2) * RHS] for e in range(count)]
        out[:, FACE1_AT : FACE1_AT + NT] = jnp.concatenate(face1, axis=0).astype(BF)


VMEM = pl.BlockSpec(memory_space=pltpu.VMEM)


def call(body, arrays, shapes, name, scratch=()):
    return pl.pallas_call(
        body,
        out_shape=[jax.ShapeDtypeStruct(s, d) for s, d in shapes],
        in_specs=[VMEM] * len(arrays),
        out_specs=[VMEM] * len(shapes),
        scratch_shapes=[pltpu.VMEM(s, d) for s, d in scratch],
        compiler_params=pltpu.CompilerParams(vmem_limit_bytes=24 * 2**20),
        name=name,
    )(*arrays)


def on_device(
    old_state, right_side, block_inverse, face_scale, sweep_level, face_source, send_list, trace_map, lift_map
):
    count, rhs, points = old_state.shape
    rows = count * rhs
    sections, parts = lax.axis_size("stream"), lax.axis_size("cross")
    axes = ("stream", "cross")
    place = jnp.stack(
        [lax.axis_index("stream"), jnp.int32(sections), lax.axis_index("cross") % 2]
    ).astype(jnp.int32).reshape(1, 3)

    def core(c):
        return c ^ 1

    def chip(c):
        return (c + 1) % parts if c % 2 else (c - 1) % parts

    def move(array, target):
        pairs = []
        for s in range(sections):
            for c in range(parts):
                to_s, to_c = target(s, c)
                pairs.append((s * parts + c, to_s * parts + to_c))
        return lax.ppermute(array, axes, pairs)

    def between(array, pair_of, across=lambda c: c):
        def target(s, c):
            other = pair_of(s)
            return (other, across(c)) if 0 <= other < sections and other != s else (s, core(c))

        return move(array, target)

    def exchange(to_core, to_chip, section=None):
        far = move(to_chip, lambda s, c: (s, chip(c) if section in (None, s) else core(c)))
        near = move(to_core, lambda s, c: (s, core(c)))
        return near, far

    message = ((CAP * rhs, NT), BF)
    held = ((rows, points), F32)
    table = (((OWN + 1) * rhs, NT), F32)
    meta, weights, state, traces, own, to_core, to_chip, face0 = call(
        prepare,
        (place, old_state.reshape(rows, points), trace_map, face_source.T, face_scale.T,
         send_list.reshape(2, CAP), sweep_level.reshape(1, count)),
        [((16, 128), jnp.int32), ((8, 128), F32), held, ((NF, points, NT), BF), table, message, message, message],
        "prepare",
    )
    first_core, first_chip = exchange(to_core, to_chip)
    inverse_t, lift, lead = call(
        turn,
        (block_inverse, lift_map.T, traces),
        [(block_inverse.shape, BF), (lift_map.shape, BF), ((count * NT, -(-points // 128) * 128), BF)],
        "turn",
    )
    right = right_side.reshape(rows, points)
    even_down = between(face0, lambda s: s ^ 1)
    odd_down = between(face0, lambda s: s + 1 if s % 2 else s - 1)
    down = jnp.where(lax.axis_index("stream") % 2 == 1, odd_down, even_down)

    def onward(array):
        return move(array, lambda s, c: ((s + 1) % sections, c))

    up_meta, up_weights = onward(meta), onward(weights)
    first_chip, up_meta, up_weights = lax.optimization_barrier((first_chip, up_meta, up_weights))
    up = face0
    whole = ((ZERO + 1) * rhs, NT), F32
    picked = (NF, rows, NT), F32
    for section in range(sections):
        from_core, from_chip = first_core, first_chip
        for level_idx in range(LEVELS - 1):
            shapes = [held, table, message, message]
            if section > 0 and level_idx == 0:
                (up,) = call(
                    functools.partial(upstream, section),
                    (up_chip, carried, up_core, meta, up, up_meta, up_weights, up_lead, lift),
                    [message],
                    "upstream",
                    scratch=[whole, picked],
                )
            arrays = (from_chip, from_core, meta, weights, state, own, up, down, right, traces, lift, inverse_t)
            outs = call(
                functools.partial(visit, section, level_idx), arrays, shapes, "visit", scratch=[whole, picked, held]
            )
            state, own = outs[0], outs[1]
            if level_idx < LEVELS - 2:
                if section == 0 and level_idx == 0:
                    lead, _ = lax.optimization_barrier((lead, own))
                    up_lead = onward(lead)
                from_core, from_chip = exchange(outs[2], outs[3], section)
        if section < sections - 1:
            pair = {section: section + 1, section + 1: section}
            up_chip = between(outs[3], lambda s: pair.get(s, s), chip)
            up_core = between(outs[2], lambda s: pair.get(s, s), core)
            (part,) = call(
                functools.partial(carry, section),
                (meta, weights, own, up, down, right, lift),
                [((rows, 512), BF)],
                "carry",
                scratch=[whole, picked],
            )
            carried = between(part, lambda s: pair.get(s, s))
    from_core, from_chip = exchange(outs[2], outs[3])
    (state,) = call(
        functools.partial(visit, None, LEVELS - 1),
        (from_chip, from_core, meta, weights, state, own, up, down, right, traces, lift, inverse_t),
        [((rows, points), BF)],
        "visit",
        scratch=[whole, picked, held],
    )
    return state.reshape(count, rhs, points)


def solution(mesh):
    return jax.shard_map(
        on_device,
        mesh=mesh,
        in_specs=(
            P(("stream", "cross"), None, None),
            P(("stream", "cross"), None, None),
            P(("stream", "cross"), None, None),
            P(("stream", "cross"), None),
            P(("stream", "cross")),
            P(("stream", "cross"), None),
            P("stream", "cross", None, None),
            P(),
            P(),
        ),
        out_specs=P(("stream", "cross"), None, None),
        check_vma=False,
    )
```

```python
import functools

import jax
import jax.numpy as jnp
from jax import lax
from jax.experimental import pallas as pl
from jax.experimental.pallas import tpu as pltpu
from jax.sharding import PartitionSpec as P

NT = 80
NF = 6
RHS = 8
LEVELS = 4
CAP = 16
OWN = 96
ZERO = 160
LISTS = 6
LEVEL_ROW = 8
PLACE_ROW = 9
GHOST_ROWS = 10
FACE1_AT = 384
BF = jnp.bfloat16
F32 = jnp.float32


def dot(a, b):
    return jnp.dot(a, b, preferred_element_type=F32)


def rounded(a):
    return a.astype(BF).astype(F32)


def block(index):
    return pl.ds(pl.multiple_of(index * RHS, RHS), RHS)


def store_own(own, state, traces):
    count = state.shape[0] // RHS
    own[OWN * RHS :] = jnp.zeros((RHS, NT), F32)
    for f in range(NF):
        rows = rounded(dot(state, traces[f]))
        for e in range(count):
            at = (e * NF + f) * RHS
            own[at : at + RHS] = rows[e * RHS : (e + 1) * RHS]


def store_sent(own, meta, *messages):
    for k, message in enumerate(messages):
        for q in range(0, CAP, 2):
            pair = [own[block(meta[LISTS + k, q + j]), :] for j in range(2)]
            message[q * RHS : (q + 2) * RHS] = jnp.concatenate(pair, axis=0).astype(BF)


def brought(sources, copies, done):
    moves = [
        pltpu.make_async_copy(source, copy, done.at[k]) for k, (source, copy) in enumerate(zip(sources, copies))
    ]
    for move in moves:
        move.start()
    return moves


def prepare(
    place, old_state, trace_map, source, scale, send, level,
    meta, weights, state, traces, own, to_core, to_chip, face0,
):
    count = level.shape[1]
    at = place[...]
    section, sections, odd = at[0, 0], at[0, 1], at[0, 2]
    row = source[...]
    first, second = (row >= 128) & (row < 144), (row >= 144) & (row < 160)
    moved = jnp.where(first, row + CAP, jnp.where(second, row - CAP, row))
    row = jnp.where(odd == 1, row, moved)
    row = jnp.where((section == 0) & (row >= 96) & (row < 112), ZERO, row)
    row = jnp.where((section == sections - 1) & (row >= 112) & (row < 128), ZERO, row)
    lists = send[...]
    lower, higher = lists[0:1], lists[1:2]
    meta[...] = jnp.zeros(meta.shape, jnp.int32)
    meta[0:NF, 0:count] = row
    meta[GHOST_ROWS : GHOST_ROWS + NF, 0:count] = jnp.where(row < 128, ZERO, row)
    meta[LISTS : LISTS + 1, 0:CAP] = jnp.where(odd == 1, lower, higher)
    meta[LISTS + 1 : LISTS + 2, 0:CAP] = jnp.where(odd == 1, higher, lower)
    meta[LEVEL_ROW : LEVEL_ROW + 1, 0:count] = level[...]
    meta[PLACE_ROW : PLACE_ROW + 1] = jnp.full((1, meta.shape[1]), section, jnp.int32)
    weights[0:NF, 0:count] = scale[...]
    current = old_state[...]
    state[...] = current.astype(F32)
    for f in range(NF):
        traces[f] = trace_map[:, f * NT : (f + 1) * NT]
    store_own(own, current, traces)
    store_sent(own, meta[...], to_core, to_chip)
    face0[...] = dot(current, traces[0]).astype(BF)


def turn(inverse_hbm, lift_hbm, traces, inverse_t, lift, lead, inverse, lift_t, done):
    count = inverse.shape[0]
    moves = brought(
        [inverse_hbm.at[e] for e in range(count)] + [lift_hbm],
        [inverse.at[e] for e in range(count)] + [lift_t],
        done,
    )
    face1 = traces[1].T
    for e in range(count):
        moves[e].wait()
        inverse_t[e] = inverse[e].T
        lead[e * NT : (e + 1) * NT, 0 : inverse.shape[2]] = dot(face1, inverse[e]).astype(BF)
    moves[count].wait()
    lift[...] = lift_t[...].T


def fill(table, start, parts):
    for k, part in enumerate(parts):
        at = (start + k * CAP) * RHS
        table[at : at + CAP * RHS] = part[...].astype(F32)


def lifted(scaled, table, lift, meta, weights, count, first=0):
    table[ZERO * RHS :] = jnp.zeros((RHS, NT), F32)
    for f in range(NF):
        for e in range(count):
            scaled[f, e * RHS : (e + 1) * RHS] = weights[f, e] * table[block(meta[first + f, e]), :]
    total = dot(scaled[0].astype(BF), lift[0:NT])
    for f in range(1, NF):
        total = total + dot(scaled[f].astype(BF), lift[f * NT : (f + 1) * NT])
    return total


def visit(
    section, level_idx, from_chip, from_core, meta_ref, weights_ref, state, own, up, down,
    right, traces, lift, inverse_t, *rest,
):
    final = section is None
    gather_all = not final and level_idx == LEVELS - 2
    *outs, table, scaled, fresh = rest
    count = inverse_t.shape[0]
    points = lift.shape[1]
    meta = meta_ref[...]

    def step():
        fill(table, OWN, (up,))
        table[0 : OWN * RHS] = own[0 : OWN * RHS]
        fill(table, OWN + CAP, (down, from_core, from_chip))
        residual = rounded(
            right[...].astype(F32) - lifted(scaled, table, lift, meta, weights_ref[...], count)
        )
        for e in range(count):
            rows = slice(e * RHS, (e + 1) * RHS)
            update = rounded(dot(residual[rows].astype(BF), inverse_t[e]))
            fresh[rows] = jnp.where(meta[LEVEL_ROW, e] == level_idx, update, state[rows])
        current = fresh[...].astype(BF)
        if final:
            outs[0][...] = current
        else:
            outs[0][...] = fresh[...]
            store_own(outs[1], current, traces)
            store_sent(outs[1], meta, outs[2], outs[3])

    if final:
        step()
        return
    active = meta[PLACE_ROW, 0] == section
    pl.when(active)(step)

    @pl.when(jnp.logical_not(active))
    def _():
        outs[0][...] = state[...]
        outs[1][...] = own[...]
        if gather_all:
            store_sent(own, meta, outs[2], outs[3])


def upstream(
    section, from_chip, carried, from_core, meta_ref, up, there_ref, weights_ref, lead, lift, out, table, scaled
):
    active = meta_ref[...][PLACE_ROW, 0] == section
    points = lift.shape[1]
    count = lead.shape[0] // NT

    @pl.when(active)
    def _():
        there = there_ref[...]
        fill(table, 128, (from_core, from_chip))
        part = carried[:, 0:points].astype(F32) - lifted(
            scaled, table, lift, there, weights_ref[...], count, GHOST_ROWS
        )
        part = rounded(part)
        before = carried[:, FACE1_AT : FACE1_AT + NT].astype(F32)
        for e in range(count):
            rows = slice(e * RHS, (e + 1) * RHS)
            update = lax.dot_general(
                part[rows].astype(BF),
                lead[e * NT : (e + 1) * NT, 0:points],
                (((1,), (1,)), ((), ())),
                preferred_element_type=F32,
            )
            table[rows] = jnp.where(there[LEVEL_ROW, e] == LEVELS - 1, rounded(update), before[rows])
        out[...] = table[0 : count * RHS].astype(BF)

    @pl.when(jnp.logical_not(active))
    def _():
        out[...] = up[...]


def carry(section, meta_ref, weights_ref, own, up, down, right, lift, out, table, scaled):
    count = right.shape[0] // RHS
    points = right.shape[1]
    meta = meta_ref[...]

    @pl.when(meta[PLACE_ROW, 0] == section)
    def _():
        table[0 : OWN * RHS] = own[0 : OWN * RHS]
        fill(table, OWN, (up, down))
        table[128 * RHS : ZERO * RHS] = jnp.zeros(((ZERO - 128) * RHS, NT), F32)
        part = right[...].astype(F32) - lifted(scaled, table, lift, meta, weights_ref[...], count)
        out[:, 0:points] = part.astype(BF)
        face1 = [own[(e * NF + 1) * RHS : (e * NF + 2) * RHS] for e in range(count)]
        out[:, FACE1_AT : FACE1_AT + NT] = jnp.concatenate(face1, axis=0).astype(BF)


VMEM = pl.BlockSpec(memory_space=pltpu.VMEM)
HBM = pl.BlockSpec(memory_space=pl.ANY)


def call(body, arrays, shapes, name, scratch=(), far=0, limit=24):
    scratch = [
        pltpu.SemaphoreType.DMA((s,)) if isinstance(s, int) else pltpu.VMEM(*s) for s in scratch
    ]
    return pl.pallas_call(
        body,
        out_shape=[jax.ShapeDtypeStruct(s, d) for s, d in shapes],
        in_specs=[HBM] * far + [VMEM] * (len(arrays) - far),
        out_specs=[VMEM] * len(shapes),
        scratch_shapes=scratch,
        compiler_params=pltpu.CompilerParams(vmem_limit_bytes=int(limit * 2**20)),
        name=name,
    )(*arrays)


def on_device(
    old_state, right_side, block_inverse, face_scale, sweep_level, face_source, send_list, trace_map, lift_map
):
    count, rhs, points = old_state.shape
    rows = count * rhs
    sections, parts = lax.axis_size("stream"), lax.axis_size("cross")
    axes = ("stream", "cross")
    place = jnp.stack(
        [lax.axis_index("stream"), jnp.int32(sections), lax.axis_index("cross") % 2]
    ).astype(jnp.int32).reshape(1, 3)

    def core(c):
        return c ^ 1

    def chip(c):
        return (c + 1) % parts if c % 2 else (c - 1) % parts

    def move(array, target):
        pairs = []
        for s in range(sections):
            for c in range(parts):
                to_s, to_c = target(s, c)
                pairs.append((s * parts + c, to_s * parts + to_c))
        return lax.ppermute(array, axes, pairs)

    def between(array, pair_of, across=lambda c: c):
        def target(s, c):
            other = pair_of(s)
            return (other, across(c)) if 0 <= other < sections and other != s else (s, core(c))

        return move(array, target)

    def exchange(to_core, to_chip, section=None):
        far = move(to_chip, lambda s, c: (s, chip(c) if section in (None, s) else core(c)))
        near = move(to_core, lambda s, c: (s, core(c)))
        return near, far

    message = ((CAP * rhs, NT), BF)
    held = ((rows, points), F32)
    table = (((OWN + 1) * rhs, NT), F32)
    inputs = (
        place, old_state.reshape(rows, points), trace_map, face_source.T, face_scale.T,
        send_list.reshape(2, CAP), sweep_level.reshape(1, count),
    )
    meta, weights, state, traces, own, to_core, to_chip, face0 = call(
        prepare,
        inputs,
        [((16, 128), jnp.int32), ((8, 128), F32), held, ((NF, points, NT), BF), table, message, message, message],
        "prepare",
    )
    first_core, first_chip = exchange(to_core, to_chip)
    inverse_t, lift, lead = call(
        turn,
        (block_inverse, lift_map.T, traces),
        [(block_inverse.shape, BF), (lift_map.shape, BF), ((count * NT, -(-points // 128) * 128), BF)],
        "turn",
        scratch=[(block_inverse.shape, BF), (lift_map.T.shape, BF), count + 1],
        far=2,
        limit=47,
    )
    right = right_side.reshape(rows, points)
    even_down = between(face0, lambda s: s ^ 1)
    odd_down = between(face0, lambda s: s + 1 if s % 2 else s - 1)
    down = jnp.where(lax.axis_index("stream") % 2 == 1, odd_down, even_down)

    def onward(array):
        return move(array, lambda s, c: ((s + 1) % sections, c))

    up = face0
    whole = ((ZERO + 1) * rhs, NT), F32
    picked = (NF, rows, NT), F32
    for section in range(sections):
        from_core, from_chip = first_core, first_chip
        for level_idx in range(LEVELS - 1):
            shapes = [held, table, message, message]
            if section > 0 and level_idx == 0:
                (up,) = call(
                    functools.partial(upstream, section),
                    (up_chip, carried, up_core, meta, up, up_meta, up_weights, up_lead, lift),
                    [message],
                    "upstream",
                    scratch=[whole, picked],
                )
            arrays = (from_chip, from_core, meta, weights, state, own, up, down, right, traces, lift, inverse_t)
            outs = call(
                functools.partial(visit, section, level_idx), arrays, shapes, "visit", scratch=[whole, picked, held]
            )
            state, own = outs[0], outs[1]
            if level_idx < LEVELS - 2:
                if section == 0 and level_idx == 0:
                    sent_meta, sent_weights, _ = lax.optimization_barrier((meta, weights, own))
                    up_meta, up_weights = onward(sent_meta), onward(sent_weights)
                elif section == 0:
                    lead, _ = lax.optimization_barrier((lead, own))
                    up_lead = onward(lead)
                from_core, from_chip = exchange(outs[2], outs[3], section)
                if section == 0 and level_idx == 0:
                    from_chip, up_meta, up_weights = lax.optimization_barrier((from_chip, up_meta, up_weights))
        if section < sections - 1:
            pair = {section: section + 1, section + 1: section}
            up_chip = between(outs[3], lambda s: pair.get(s, s), chip)
            up_core = between(outs[2], lambda s: pair.get(s, s), core)
            (part,) = call(
                functools.partial(carry, section),
                (meta, weights, own, up, down, right, lift),
                [((rows, 512), BF)],
                "carry",
                scratch=[whole, picked],
            )
            carried = between(part, lambda s: pair.get(s, s))
    from_core, from_chip = exchange(outs[2], outs[3])
    (state,) = call(
        functools.partial(visit, None, LEVELS - 1),
        (from_chip, from_core, meta, weights, state, own, up, down, right, traces, lift, inverse_t),
        [((rows, points), BF)],
        "visit",
        scratch=[whole, picked, held],
    )
    return state.reshape(count, rhs, points)


def solution(mesh):
    return jax.shard_map(
        on_device,
        mesh=mesh,
        in_specs=(
            P(("stream", "cross"), None, None),
            P(("stream", "cross"), None, None),
            P(("stream", "cross"), None, None),
            P(("stream", "cross"), None),
            P(("stream", "cross")),
            P(("stream", "cross"), None),
            P("stream", "cross", None, None),
            P(),
            P(),
        ),
        out_specs=P(("stream", "cross"), None, None),
        check_vma=False,
    )
```

```python
import functools

import jax
import jax.numpy as jnp
from jax import lax
from jax.experimental import pallas as pl
from jax.experimental.pallas import tpu as pltpu
from jax.sharding import PartitionSpec as P

NT = 80
NF = 6
RHS = 8
LEVELS = 4
CAP = 16
OWN = 96
ZERO = 160
LISTS = 6
LEVEL_ROW = 8
PLACE_ROW = 9
GHOST_ROWS = 10
FACE1_AT = 384
BF = jnp.bfloat16
F32 = jnp.float32


def dot(a, b):
    return jnp.dot(a, b, preferred_element_type=F32)


def rounded(a):
    return a.astype(BF).astype(F32)


def block(index):
    return pl.ds(pl.multiple_of(index * RHS, RHS), RHS)


def store_own(own, state, traces):
    count = state.shape[0] // RHS
    own[OWN * RHS :] = jnp.zeros((RHS, NT), F32)
    for f in range(NF):
        rows = rounded(dot(state, traces[f]))
        for e in range(count):
            at = (e * NF + f) * RHS
            own[at : at + RHS] = rows[e * RHS : (e + 1) * RHS]


def store_sent(own, meta, *messages):
    for k, message in enumerate(messages):
        for q in range(0, CAP, 2):
            pair = [own[block(meta[LISTS + k, q + j]), :] for j in range(2)]
            message[q * RHS : (q + 2) * RHS] = jnp.concatenate(pair, axis=0).astype(BF)


def prepare(
    place, old_state, trace_map, source, scale, send, level,
    meta, weights, state, traces, own, to_core, to_chip, face0,
):
    count = level.shape[1]
    at = place[...]
    section, sections, odd = at[0, 0], at[0, 1], at[0, 2]
    row = source[...]
    first, second = (row >= 128) & (row < 144), (row >= 144) & (row < 160)
    moved = jnp.where(first, row + CAP, jnp.where(second, row - CAP, row))
    row = jnp.where(odd == 1, row, moved)
    row = jnp.where((section == 0) & (row >= 96) & (row < 112), ZERO, row)
    row = jnp.where((section == sections - 1) & (row >= 112) & (row < 128), ZERO, row)
    lists = send[...]
    lower, higher = lists[0:1], lists[1:2]
    meta[...] = jnp.zeros(meta.shape, jnp.int32)
    meta[0:NF, 0:count] = row
    meta[GHOST_ROWS : GHOST_ROWS + NF, 0:count] = jnp.where(row < 128 + CAP, ZERO, row)
    meta[LISTS : LISTS + 1, 0:CAP] = jnp.where(odd == 1, lower, higher)
    meta[LISTS + 1 : LISTS + 2, 0:CAP] = jnp.where(odd == 1, higher, lower)
    meta[LEVEL_ROW : LEVEL_ROW + 1, 0:count] = level[...]
    meta[PLACE_ROW : PLACE_ROW + 1] = jnp.full((1, meta.shape[1]), section, jnp.int32)
    weights[0:NF, 0:count] = scale[...]
    current = old_state[...]
    state[...] = current.astype(F32)
    for f in range(NF):
        traces[f] = trace_map[:, f * NT : (f + 1) * NT]
    store_own(own, current, traces)
    store_sent(own, meta[...], to_core, to_chip)
    face0[...] = dot(current, traces[0]).astype(BF)


def turn(inverse, lift_t, traces, inverse_t, lift, lead):
    face1 = traces[1].T
    for e in range(inverse.shape[0]):
        inverse_t[e] = inverse[e].T
        lead[e * NT : (e + 1) * NT, 0 : inverse.shape[2]] = dot(face1, inverse[e]).astype(BF)
    lift[...] = lift_t[...].T


def fill(table, start, parts):
    for k, part in enumerate(parts):
        at = (start + k * CAP) * RHS
        table[at : at + CAP * RHS] = part[...].astype(F32)


def lifted(scaled, table, lift, meta, weights, count, first=0):
    table[ZERO * RHS :] = jnp.zeros((RHS, NT), F32)
    for f in range(NF):
        for e in range(count):
            scaled[f, e * RHS : (e + 1) * RHS] = weights[f, e] * table[block(meta[first + f, e]), :]
    total = dot(scaled[0].astype(BF), lift[0:NT])
    for f in range(1, NF):
        total = total + dot(scaled[f].astype(BF), lift[f * NT : (f + 1) * NT])
    return total


def visit(
    section, level_idx, from_chip, from_core, meta_ref, weights_ref, state, own, up, down,
    right, traces, lift, inverse_t, *rest,
):
    final = section is None
    gather_all = not final and level_idx == LEVELS - 2
    *outs, table, scaled, fresh = rest
    count = inverse_t.shape[0]
    points = lift.shape[1]
    meta = meta_ref[...]

    def step():
        fill(table, OWN, (up,))
        table[0 : OWN * RHS] = own[0 : OWN * RHS]
        fill(table, OWN + CAP, (down, from_core, from_chip))
        residual = rounded(
            right[...].astype(F32) - lifted(scaled, table, lift, meta, weights_ref[...], count)
        )
        for e in range(count):
            rows = slice(e * RHS, (e + 1) * RHS)
            update = rounded(dot(residual[rows].astype(BF), inverse_t[e]))
            fresh[rows] = jnp.where(meta[LEVEL_ROW, e] == level_idx, update, state[rows])
        current = fresh[...].astype(BF)
        if final:
            outs[0][...] = current
        else:
            outs[0][...] = fresh[...]
            store_own(outs[1], current, traces)
            store_sent(outs[1], meta, outs[2], outs[3])

    if final:
        step()
        return
    active = meta[PLACE_ROW, 0] == section
    pl.when(active)(step)

    @pl.when(jnp.logical_not(active))
    def _():
        outs[0][...] = state[...]
        outs[1][...] = own[...]
        if gather_all:
            store_sent(own, meta, outs[2], outs[3])


def upstream(
    section, from_chip, carried, meta_ref, up, there_ref, weights_ref, lead, lift, out, table, scaled
):
    active = meta_ref[...][PLACE_ROW, 0] == section
    points = lift.shape[1]
    count = lead.shape[0] // NT

    @pl.when(active)
    def _():
        there = there_ref[...]
        fill(table, 128 + CAP, (from_chip,))
        part = carried[:, 0:points].astype(F32) - lifted(
            scaled, table, lift, there, weights_ref[...], count, GHOST_ROWS
        )
        part = rounded(part)
        before = carried[:, FACE1_AT : FACE1_AT + NT].astype(F32)
        for e in range(count):
            rows = slice(e * RHS, (e + 1) * RHS)
            update = lax.dot_general(
                part[rows].astype(BF),
                lead[e * NT : (e + 1) * NT, 0:points],
                (((1,), (1,)), ((), ())),
                preferred_element_type=F32,
            )
            table[rows] = jnp.where(there[LEVEL_ROW, e] == LEVELS - 1, rounded(update), before[rows])
        out[...] = table[0 : count * RHS].astype(BF)

    @pl.when(jnp.logical_not(active))
    def _():
        out[...] = up[...]


def carry(section, from_core, meta_ref, weights_ref, own, up, down, right, lift, out, table, scaled):
    count = right.shape[0] // RHS
    points = right.shape[1]
    meta = meta_ref[...]

    @pl.when(meta[PLACE_ROW, 0] == section)
    def _():
        table[0 : OWN * RHS] = own[0 : OWN * RHS]
        fill(table, OWN, (up, down, from_core))
        table[(128 + CAP) * RHS : ZERO * RHS] = jnp.zeros((CAP * RHS, NT), F32)
        part = right[...].astype(F32) - lifted(scaled, table, lift, meta, weights_ref[...], count)
        out[:, 0:points] = part.astype(BF)
        face1 = [own[(e * NF + 1) * RHS : (e * NF + 2) * RHS] for e in range(count)]
        out[:, FACE1_AT : FACE1_AT + NT] = jnp.concatenate(face1, axis=0).astype(BF)


VMEM = pl.BlockSpec(memory_space=pltpu.VMEM)


def call(body, arrays, shapes, name, scratch=()):
    return pl.pallas_call(
        body,
        out_shape=[jax.ShapeDtypeStruct(s, d) for s, d in shapes],
        in_specs=[VMEM] * len(arrays),
        out_specs=[VMEM] * len(shapes),
        scratch_shapes=[pltpu.VMEM(s, d) for s, d in scratch],
        compiler_params=pltpu.CompilerParams(vmem_limit_bytes=24 * 2**20),
        name=name,
    )(*arrays)


def on_device(
    old_state, right_side, block_inverse, face_scale, sweep_level, face_source, send_list, trace_map, lift_map
):
    count, rhs, points = old_state.shape
    rows = count * rhs
    sections, parts = lax.axis_size("stream"), lax.axis_size("cross")
    axes = ("stream", "cross")
    place = jnp.stack(
        [lax.axis_index("stream"), jnp.int32(sections), lax.axis_index("cross") % 2]
    ).astype(jnp.int32).reshape(1, 3)

    def core(c):
        return c ^ 1

    def chip(c):
        return (c + 1) % parts if c % 2 else (c - 1) % parts

    def move(array, target):
        pairs = []
        for s in range(sections):
            for c in range(parts):
                to_s, to_c = target(s, c)
                pairs.append((s * parts + c, to_s * parts + to_c))
        return lax.ppermute(array, axes, pairs)

    def between(array, pair_of, across=lambda c: c):
        def target(s, c):
            other = pair_of(s)
            return (other, across(c)) if 0 <= other < sections and other != s else (s, core(c))

        return move(array, target)

    def exchange(to_core, to_chip, section=None):
        far = move(to_chip, lambda s, c: (s, chip(c) if section in (None, s) else core(c)))
        near = move(to_core, lambda s, c: (s, core(c)))
        return near, far

    message = ((CAP * rhs, NT), BF)
    held = ((rows, points), F32)
    table = (((OWN + 1) * rhs, NT), F32)
    meta, weights, state, traces, own, to_core, to_chip, face0 = call(
        prepare,
        (place, old_state.reshape(rows, points), trace_map, face_source.T, face_scale.T,
         send_list.reshape(2, CAP), sweep_level.reshape(1, count)),
        [((16, 128), jnp.int32), ((8, 128), F32), held, ((NF, points, NT), BF), table, message, message, message],
        "prepare",
    )
    first_core, first_chip = exchange(to_core, to_chip)
    inverse_t, lift, lead = call(
        turn,
        (block_inverse, lift_map.T, traces),
        [(block_inverse.shape, BF), (lift_map.shape, BF), ((count * NT, -(-points // 128) * 128), BF)],
        "turn",
    )
    right = right_side.reshape(rows, points)
    even_down = between(face0, lambda s: s ^ 1)
    odd_down = between(face0, lambda s: s + 1 if s % 2 else s - 1)
    down = jnp.where(lax.axis_index("stream") % 2 == 1, odd_down, even_down)

    def onward(array):
        return move(array, lambda s, c: ((s + 1) % sections, c))

    up = face0
    whole = ((ZERO + 1) * rhs, NT), F32
    picked = (NF, rows, NT), F32
    for section in range(sections):
        from_core, from_chip = first_core, first_chip
        for level_idx in range(LEVELS - 1):
            shapes = [held, table, message, message]
            if section > 0 and level_idx == 0:
                (up,) = call(
                    functools.partial(upstream, section),
                    (up_chip, carried, meta, up, up_meta, up_weights, up_lead, lift),
                    [message],
                    "upstream",
                    scratch=[whole, picked],
                )
            arrays = (from_chip, from_core, meta, weights, state, own, up, down, right, traces, lift, inverse_t)
            outs = call(
                functools.partial(visit, section, level_idx), arrays, shapes, "visit", scratch=[whole, picked, held]
            )
            state, own = outs[0], outs[1]
            if level_idx < LEVELS - 2:
                if section == 0 and level_idx == 0:
                    sent_meta, sent_weights, _ = lax.optimization_barrier((meta, weights, own))
                    up_meta, up_weights = onward(sent_meta), onward(sent_weights)
                    lead, up_meta, up_weights = lax.optimization_barrier((lead, up_meta, up_weights))
                    up_lead = onward(lead)
                from_core, from_chip = exchange(outs[2], outs[3], section)
        if section < sections - 1:
            others = [s for s in range(sections) if s not in (section, section + 1)]

            def ahead(array, across, back):
                def target(s, c):
                    if s == section:
                        return section + 1, across(c)
                    if s == section + 1:
                        return back, c
                    return (section, c) if s == back else (s, core(c))

                return move(array, target)

            up_chip = ahead(outs[3], chip, others[0])
            beside = move(outs[2], lambda s, c: (s, core(c)))
            (part,) = call(
                functools.partial(carry, section),
                (beside, meta, weights, own, up, down, right, lift),
                [((rows, 512), BF)],
                "carry",
                scratch=[whole, picked],
            )
            carried = ahead(part, lambda c: c, others[1])
    from_core, from_chip = exchange(outs[2], outs[3])
    (state,) = call(
        functools.partial(visit, None, LEVELS - 1),
        (from_chip, from_core, meta, weights, state, own, up, down, right, traces, lift, inverse_t),
        [((rows, points), BF)],
        "visit",
        scratch=[whole, picked, held],
    )
    return state.reshape(count, rhs, points)


def solution(mesh):
    return jax.shard_map(
        on_device,
        mesh=mesh,
        in_specs=(
            P(("stream", "cross"), None, None),
            P(("stream", "cross"), None, None),
            P(("stream", "cross"), None, None),
            P(("stream", "cross"), None),
            P(("stream", "cross")),
            P(("stream", "cross"), None),
            P("stream", "cross", None, None),
            P(),
            P(),
        ),
        out_specs=P(("stream", "cross"), None, None),
        check_vma=False,
    )
```
